32 devices in a mesh: expert: 16 (over z, y, x), fsdp: 2 (over core).
Axes of the slice: x: 2, y: 2, z: 4, core: 2. Of those that a mesh axis runs over, the one named last changes fastest.
Arguments:
- out_grad: bfloat16 [2048, 2560], P('expert', 'fsdp'), may hold values from -6 to 6
- expert_ids: int32 [2048, 6], P('expert'), may hold values from 0 to 15, all different within a row; in each aligned block of 128 rows (0 to 127, 128 to 255, ...) at most 72 rows name the same one
- gate_probs: float32 [2048, 6], P('expert'), may hold values from 0.02 to 0.6
- saved_inputs: bfloat16 [16, 1152, 2560], P('expert', 'fsdp'), may hold values from -6 to 6
- gate_weight: bfloat16 [16, 2560, 768], P('expert', 'fsdp'), may hold values from -0.125 to 0.125
- up_weight: bfloat16 [16, 2560, 768], P('expert', 'fsdp'), may hold values from -0.125 to 0.125
- down_weight: bfloat16 [16, 2560, 768], P('expert', 'fsdp'), may hold values from -0.21875 to 0.21875
Outputs:
- input_grad: bfloat16 [2048, 2560], P('expert', 'fsdp')
- gate_grad: bfloat16 [2048, 6], P('expert')
- down_grad: float32 [16, 2560, 768], P('expert', 'fsdp')
The draws below stay inside these ranges and needn't reach their ends.
Inputs may be any that keep to these rules, and one draw needn't show every extreme that they name: `expert_ids`: each row names 6 different experts. The rows of one block of 128 tokens name any one expert at most 72 times, and in every draw the rows of some block name some expert exactly 72 times.
All inputs are finite; a program needn't handle non-finite values.
Results may differ from the reference program's by a relative error of at most 0.011.
Values may be sent and summed in bfloat16 or wider, within the bound.
No kernel may reach another device: no remote copies, remote signals or barrier semaphores. Data moves between devices by JAX's collectives and lax.ppermute only.
A program may use at most 128 MiB of HBM per device.

```python
import math
import jax
import jax.numpy as jnp
import numpy as np
from jax import lax

D = 2560
H = 768
TOPK = 6
TOK_DEV = 128
EXPERTS = 16
CAP = 72
SLOTS = 1152
TOKENS = 2048


def level_of(rng, extent, shards, least, largest):
    loudness, own = 1.0, jax.random.fold_in(rng, 6)
    for position, shards_of in shards:
        steps = jnp.exp(jax.random.uniform(jax.random.fold_in(own, position), (shards_of,), jnp.float32, least / len(shards), largest / len(shards)))
        loudness = loudness * jnp.repeat(steps, extent[position] // shards_of).reshape([-1 if axis == position else 1 for axis in range(len(extent))])
    return loudness


def routed_block(own_key, own, number, rows, amount, top, reach, skew):
    ranking = jax.random.permutation(own_key, amount)
    heavy_load, usual = load_shares(amount, rows * top, reach, skew, True), load_shares(amount, rows * top, reach, skew, False)
    places = jnp.arange(amount)

    def named(tallies, rotation):
        used = int((tallies > 0).sum())
        fixed = max(1, used // 4)
        shifted = fixed + (places - fixed + rotation * (used - fixed)) % max(1, amount - fixed)
        return jnp.zeros((amount,), jnp.int32).at[ranking[jnp.where(places < fixed, places, shifted)]].set(jnp.asarray(tallies, jnp.int32))

    tallies = jnp.where(number % 4 == 0, named(heavy_load, number // 4), named(usual, number - number // 4 - 1))
    mixed = jax.random.permutation(jax.random.fold_in(own, 3), amount)
    donor, sink = mixed[0:amount // 2 * 2:2], mixed[1:amount // 2 * 2:2]
    margin = jnp.minimum(tallies[donor] - 1, reach - tallies[sink]) // 2
    margin = jnp.where((donor == ranking[0]) | (sink == ranking[0]) | (tallies[sink] == 0), 0, jnp.maximum(margin, 0))
    shifted = jax.random.randint(jax.random.fold_in(own, 4), (amount // 2,), 0, 1 << 20) % (margin + 1)
    tallies = tallies.at[donor].add(-shifted).at[sink].add(shifted)
    members = jnp.searchsorted(jnp.cumsum(tallies), jnp.arange(rows * top), side="right").astype(jnp.int32)
    table = members.reshape(top, rows).T
    table = table[jax.random.permutation(jax.random.fold_in(own, 1), rows)]
    rotation = jax.random.randint(jax.random.fold_in(own, 2), (rows, 1), 0, top)
    return jnp.take_along_axis(table, (jnp.arange(top)[None, :] + rotation) % top, axis=1)


def load_shares(count, total, bound, lean, full):
    loads = [(1 << 20) // math.isqrt(standing ** lean) + 1 for standing in range(1, count + 1)]
    largest = bound if full else min(bound, max(-(-total // count), total * loads[0] // sum(loads)))
    least = 1 if total - largest >= count - 1 else 0
    holding, rest = [largest] + [least] * (count - 1), total - largest - least * (count - 1)
    while rest > 0:
        candidates = [i for i in range(1, count) if holding[i] < largest] or [i for i in range(1, count) if holding[i] < bound]
        mass, left = sum([loads[i] for i in candidates]), rest
        for i in candidates:
            extra = min(bound - holding[i], max(1, left * loads[i] // mass), rest)
            holding[i] = holding[i] + extra
            rest = rest - extra
    return np.array(holding)


def bell_draw(rng, extent, scale, most, shards=(), kind=jnp.bfloat16):
    array = scale * jax.random.normal(rng, extent, jnp.float32)
    if shards:
        array = array * level_of(rng, extent, shards, -0.22, 0.18)
    return jnp.clip(array, -most, most).astype(kind)


def setup_inputs(seed: int = 0) -> dict:
    keys = jax.random.split(jax.random.key(seed), 8)
    out_grad = bell_draw(keys[0], (TOKENS, D), 1.0, 6.0, ((0, 16), (1, 2)))
    expert_ids_keys = jax.random.split(jax.random.fold_in(keys[1], 1), TOKENS // TOK_DEV)
    expert_ids_turns = jax.random.permutation(jax.random.fold_in(keys[1], 3), TOKENS // TOK_DEV)
    expert_ids = jax.vmap(lambda own, number: routed_block(jax.random.fold_in(keys[1], 2), own, number, TOK_DEV, EXPERTS, TOPK, CAP, 2))(expert_ids_keys, expert_ids_turns).reshape((TOKENS, TOPK))
    gate_probs = jnp.clip(jnp.exp(math.log(0.6) - 3.4011974 * jax.random.uniform(keys[2], (TOKENS, TOPK), jnp.float32) ** level_of(keys[2], (TOKENS, TOPK), ((0, 16),), -0.2, 0.2)), 0.02, 0.6)
    saved_inputs = bell_draw(keys[3], (EXPERTS, SLOTS, D), 1.0, 6.0, ((0, 16), (1, 2)))
    gate_weight = bell_draw(keys[4], (EXPERTS, D, H), D ** -0.5, 0.125, ((0, 16), (1, 2)))
    up_weight = bell_draw(keys[5], (EXPERTS, D, H), D ** -0.5, 0.125, ((0, 16), (1, 2)))
    down_weight = bell_draw(keys[6], (EXPERTS, D, H), H ** -0.5, 0.21875, ((0, 16), (1, 2)))
    return {"out_grad": out_grad, "expert_ids": expert_ids, "gate_probs": gate_probs, "saved_inputs": saved_inputs, "gate_weight": gate_weight, "up_weight": up_weight, "down_weight": down_weight}


def reference(out_grad, expert_ids, gate_probs, saved_inputs, gate_weight, up_weight, down_weight):
    token_count, model_width = out_grad.shape
    top_count = expert_ids.shape[1]
    expert_count = gate_weight.shape[0]
    slot_count = saved_inputs.shape[1]
    route_count = token_count * top_count
    block_count = token_count // TOK_DEV
    block_ids = expert_ids.reshape(block_count, TOK_DEV * top_count)
    route_table = (block_ids[:, :, None] == jnp.arange(expert_count, dtype=jnp.int32)[None, None, :]).astype(jnp.int32)
    earlier = jnp.cumsum(route_table, axis=1) - route_table
    route_rank = jnp.sum(earlier * route_table, axis=2).astype(jnp.int32)
    block_index = jnp.arange(block_count, dtype=jnp.int32)
    route_row = (block_index[:, None] * CAP + route_rank).reshape(route_count).astype(jnp.int32)
    flat_ids = expert_ids.reshape(route_count)
    route_index = jnp.arange(route_count, dtype=jnp.int32)
    token_of_route = route_index // top_count
    probs_half = gate_probs.reshape(route_count).astype(jnp.bfloat16)

    def one_expert(carried, expert_index):
        input_sum, gate_slots = carried
        target = jnp.where(flat_ids == expert_index, route_row, slot_count).astype(jnp.int32)
        token_at = jnp.zeros((slot_count,), jnp.int32).at[target].set(token_of_route, mode="drop")
        route_at = jnp.zeros((slot_count,), jnp.int32).at[target].set(route_index, mode="drop")
        live_slot = jnp.zeros((slot_count,), jnp.bool_).at[target].set(True, mode="drop")
        grad_rows = jnp.where(live_slot[:, None], out_grad[token_at], jnp.zeros((), jnp.bfloat16))
        prob_rows = jnp.where(live_slot, probs_half[route_at], jnp.zeros((), jnp.bfloat16)).astype(jnp.float32)
        inputs = saved_inputs[expert_index]
        gate_full = gate_weight[expert_index]
        up_full = up_weight[expert_index]
        down_full = down_weight[expert_index]
        gate_pre = jnp.dot(inputs, gate_full, preferred_element_type=jnp.float32)
        up_pre = jnp.dot(inputs, up_full, preferred_element_type=jnp.float32)
        hidden = (jax.nn.silu(gate_pre) * up_pre).astype(jnp.bfloat16)
        raw_grad = jnp.dot(grad_rows, down_full, preferred_element_type=jnp.float32)
        slot_gate = jnp.sum(raw_grad * hidden.astype(jnp.float32), axis=1).astype(jnp.bfloat16)
        scaled_grad = (prob_rows[:, None] * grad_rows.astype(jnp.float32)).astype(jnp.bfloat16)
        down_grad = jnp.dot(scaled_grad.T, hidden, preferred_element_type=jnp.float32)
        hidden_grad = prob_rows[:, None] * raw_grad
        sigmoid_gate = jax.nn.sigmoid(gate_pre)
        gate_pre_grad = (hidden_grad * up_pre * sigmoid_gate * (1.0 + gate_pre * (1.0 - sigmoid_gate))).astype(jnp.bfloat16)
        up_pre_grad = (hidden_grad * jax.nn.silu(gate_pre)).astype(jnp.bfloat16)
        slot_input = (
            jnp.dot(gate_pre_grad, gate_full.T, preferred_element_type=jnp.float32)
            + jnp.dot(up_pre_grad, up_full.T, preferred_element_type=jnp.float32)
        ).astype(jnp.bfloat16)
        gate_slots = gate_slots.at[jnp.where(live_slot, route_at, route_count).astype(jnp.int32)].set(slot_gate, mode="drop")
        input_sum = input_sum.at[jnp.where(live_slot, token_at, token_count).astype(jnp.int32)].add(slot_input.astype(jnp.float32), mode="drop")
        return (input_sum, gate_slots), down_grad

    initial = (jnp.zeros((token_count, model_width), jnp.float32), jnp.zeros((route_count,), jnp.bfloat16))
    (input_sum, gate_slots), down_grad = lax.scan(one_expert, initial, jnp.arange(expert_count, dtype=jnp.int32))
    return input_sum.astype(jnp.bfloat16), gate_slots.reshape(token_count, top_count), down_grad
```

```python
import jax
import jax.numpy as jnp
from jax import lax
from jax.sharding import PartitionSpec as P

LAYERS = 4
GROUPS = ((0,), (1,), (2,), (3,))
RETURN = (2, 3, 1, 0)


def body(out_grad, expert_ids, gate_probs, saved_inputs, gate_weight, up_weight, down_weight):
    bf16, f32 = jnp.bfloat16, jnp.float32
    tokens, width = out_grad.shape
    top = expert_ids.shape[1]
    experts = lax.axis_size("expert")
    plane = experts // LAYERS
    local_rows = saved_inputs.shape[1]
    slots = local_rows * lax.axis_size("fsdp")
    depth = slots // experts
    hidden_units = gate_weight.shape[2]
    me = lax.axis_index("expert")
    core = lax.axis_index("fsdp")
    layer, spot = me // plane, me % plane

    def other_core(array):
        return lax.ppermute(array, "fsdp", [(0, 1), (1, 0)])

    def other_layer(array, r):
        return lax.ppermute(array, "expert", [(e, e ^ (r * plane)) for e in range(experts)])

    def other_spot(array, o):
        return lax.ppermute(array, "expert", [(e, e ^ o) for e in range(experts)])

    ids_row = expert_ids.astype(bf16).T.reshape(1, top * tokens)
    prob_row = gate_probs.astype(bf16).T.reshape(1, top * tokens)
    routes = jnp.pad(
        jnp.concatenate([ids_row, prob_row]), ((0, 14), (0, width - top * tokens))
    )
    payload = jnp.concatenate([out_grad, routes])
    blocks = [payload]
    for r in range(1, LAYERS):
        blocks.append(other_layer(payload, r))

    gate_other = other_core(gate_weight[0])
    up_other = other_core(up_weight[0])

    order = jnp.arange(tokens)
    before = (order[:, None] < order[None, :]).astype(bf16)

    def tables(block):
        ids = block[tokens, : top * tokens].reshape(top, tokens).astype(f32)
        probs = block[tokens + 1, : top * tokens].reshape(top, tokens).astype(f32)
        offsets = jnp.arange(plane, dtype=jnp.int32)
        named = (layer * plane + (spot ^ offsets)).astype(f32)
        hit = ids[None] == named[:, None, None]
        member = jnp.any(hit, axis=1)
        prob = jnp.sum(jnp.where(hit, probs[None], 0.0), axis=1)
        rank = jnp.dot(member.astype(bf16), before, preferred_element_type=f32)
        rows = jnp.arange(depth, dtype=jnp.int32).astype(f32)
        chosen = (rank[:, None, :] == rows[None, :, None]) & member[:, None, :]
        return chosen.astype(bf16), jnp.where(chosen, prob[:, None, :], 0.0).astype(bf16)

    chosen, arrived = [], []
    for r in range(LAYERS):
        pick, weighted = tables(blocks[r])
        chosen.append(pick)
        parts = []
        for o in range(plane):
            rows = jnp.dot(
                weighted[o], blocks[r][:tokens], preferred_element_type=f32
            ).astype(bf16)
            parts.append(rows if o == 0 else other_spot(rows, o))
        held = jnp.zeros((plane, depth, width), bf16)
        for o in range(plane):
            held = lax.dynamic_update_slice(held, parts[o][None], (spot ^ o, 0, 0))
        arrived.append(held.reshape(plane * depth, width))

    inputs = saved_inputs[0]
    mine = lax.dynamic_slice_in_dim(inputs, core * width, width, 1)
    theirs = lax.dynamic_slice_in_dim(inputs, (1 - core) * width, width, 1)
    gate_pre = jnp.dot(mine, gate_weight[0], preferred_element_type=f32) + jnp.dot(
        theirs, gate_other, preferred_element_type=f32
    )
    up_pre = jnp.dot(mine, up_weight[0], preferred_element_type=f32) + jnp.dot(
        theirs, up_other, preferred_element_type=f32
    )
    sig = jax.nn.sigmoid(gate_pre)
    silu = gate_pre * sig
    factors = jnp.stack(
        [
            (silu * up_pre).astype(bf16),
            (up_pre * sig * (1.0 + gate_pre * (1.0 - sig))).astype(bf16),
            silu.astype(bf16),
        ]
    ).reshape(3, LAYERS // 2, plane * depth, hidden_units)
    factors_other = other_core(factors)
    factors_all = jnp.where(
        core == 0,
        jnp.concatenate([factors, factors_other], 1),
        jnp.concatenate([factors_other, factors], 1),
    )

    slot_input, slot_gate = [], jnp.zeros((LAYERS, plane * depth), bf16)
    for r in range(LAYERS):
        part = jnp.dot(arrived[r], down_weight[0], preferred_element_type=f32)
        hidden_grad = part + other_core(part.astype(bf16)).astype(f32)
        here = lax.dynamic_index_in_dim(factors_all, layer ^ r, 1, keepdims=False).astype(f32)
        slot_gate = lax.dynamic_update_slice(
            slot_gate, jnp.sum(hidden_grad * here[0], 1).astype(bf16)[None], (layer ^ r, 0)
        )
        gate_pre_grad = (hidden_grad * here[1]).astype(bf16)
        up_pre_grad = (hidden_grad * here[2]).astype(bf16)
        last = (((1,), (1,)), ((), ()))
        slot_input.append(
            (
                lax.dot_general(gate_pre_grad, gate_weight[0], last, preferred_element_type=f32)
                + lax.dot_general(up_pre_grad, up_weight[0], last, preferred_element_type=f32)
            )
            .astype(bf16)
            .reshape(plane, depth, width)
        )

    home = [None] * LAYERS
    for r in RETURN:
        back = []
        for o in range(plane):
            rows = lax.dynamic_index_in_dim(slot_input[r], spot ^ o, 0, keepdims=False)
            back.append(rows if o == 0 else other_spot(rows, o))
        total = lax.dot_general(
            chosen[r].reshape(plane * depth, tokens),
            jnp.concatenate(back),
            (((0,), (0,)), ((), ())),
            preferred_element_type=f32,
        )
        home[r] = total if r == 0 else other_layer(total.astype(bf16), r).astype(f32)
    input_grad = (home[0] + home[1] + home[2] + home[3]).astype(bf16)

    gate_slots = lax.all_gather(slot_gate.reshape(slots), "expert", axis=0)
    gate_mine = lax.dynamic_slice_in_dim(gate_slots, me * depth, depth, 1)
    flat = expert_ids.reshape(tokens * top)
    named = flat[:, None] == jnp.arange(experts, dtype=jnp.int32)[None, :]
    member = jnp.any(named.reshape(tokens, top, experts), axis=1).astype(bf16)
    earlier = jnp.dot(before.T, member, preferred_element_type=f32)
    rank = jnp.sum(
        jnp.where(named.reshape(tokens, top, experts), earlier[:, None, :], 0.0), axis=2
    ).reshape(tokens * top)
    rows = jnp.dot(named.astype(bf16), gate_mine, preferred_element_type=f32)
    here = rank[:, None] == jnp.arange(depth, dtype=jnp.int32).astype(f32)[None, :]
    routed = jnp.sum(jnp.where(here, rows, 0.0), axis=1).reshape(tokens, top)
    gate_grad = (routed / gate_probs.astype(bf16).astype(f32)).astype(bf16)

    natural = jnp.zeros((LAYERS, plane * depth, width), bf16)
    for r in range(LAYERS):
        natural = lax.dynamic_update_slice(natural, arrived[r][None], (layer ^ r, 0, 0))
    down_grad = lax.dot_general(
        natural.reshape(slots, width),
        factors_all[0].reshape(slots, hidden_units),
        (((0,), (0,)), ((), ())),
        preferred_element_type=f32,
    )
    return input_grad, gate_grad, down_grad[None]


def solution(mesh):
    return jax.shard_map(
        body,
        mesh=mesh,
        in_specs=(
            P("expert", "fsdp"),
            P("expert", None),
            P("expert", None),
            P("expert", "fsdp", None),
            P("expert", "fsdp", None),
            P("expert", "fsdp", None),
            P("expert", "fsdp", None),
        ),
        out_specs=(P("expert", "fsdp"), P("expert", None), P("expert", "fsdp", None)),
        check_vma=False,
    )
```

```python
import functools
import jax
import jax.numpy as jnp
from jax import lax
from jax.experimental import pallas as pl
from jax.experimental.pallas import tpu as pltpu
from jax.sharding import PartitionSpec as P

LAYERS = 4
META = 16
TILE = 256
BF16, F32 = jnp.bfloat16, jnp.float32
ROWS_ROWS = (((0,), (0,)), ((), ()))
COLS_COLS = (((1,), (1,)), ((), ()))
VMEM = pl.BlockSpec(memory_space=pltpu.VMEM)
SMEM = pl.BlockSpec(memory_space=pltpu.SMEM)
ANY = pl.BlockSpec(memory_space=pl.ANY)


def dot(a, b, dims=(((1,), (0,)), ((), ()))):
    return lax.dot_general(a, b, dims, preferred_element_type=F32)


def stacked(refs):
    return jnp.concatenate([ref.astype(F32) for ref in refs], 0).astype(BF16)


def params(mib=24):
    return pltpu.CompilerParams(vmem_limit_bytes=mib * 1024 * 1024)


def pack_kernel(ids_ref, probs_ref, tok_ref, out_ref):
    tokens, top = ids_ref.shape
    width = tok_ref.shape[1]
    eye = (
        lax.broadcasted_iota(jnp.int32, (tokens, tokens), 0)
        == lax.broadcasted_iota(jnp.int32, (tokens, tokens), 1)
    ).astype(BF16)
    ids = dot(ids_ref[...].astype(F32).astype(BF16), eye, ROWS_ROWS)
    probs = dot(probs_ref[...].astype(BF16), eye, ROWS_ROWS)
    none = jnp.full((8 - top, tokens), -1.0, F32)
    meta = jnp.concatenate([ids, none, probs, none], 0).astype(BF16)
    out_ref[0:tokens, :] = tok_ref[...]
    out_ref[tokens : tokens + META, :] = jnp.zeros((META, width), BF16)
    out_ref[tokens : tokens + META, 0:tokens] = meta


def slot_tables(ids, probs, experts, depth, scratch):
    tokens = ids.shape[1]
    scratch[...] = jnp.zeros_like(scratch)
    weights = []
    for i, expert in enumerate(experts):
        hit = ids == expert.astype(F32)
        scratch[i : i + 1, :] = jnp.max(jnp.where(hit, 1.0, 0.0), axis=0, keepdims=True)
        weights.append(jnp.sum(jnp.where(hit, probs, 0.0), axis=0, keepdims=True))
    before = (
        lax.broadcasted_iota(jnp.int32, (tokens, tokens), 0)
        < lax.broadcasted_iota(jnp.int32, (tokens, tokens), 1)
    ).astype(BF16)
    member = scratch[...]
    rank = jnp.where(member > 0.5, dot(member.astype(BF16), before), -1.0)
    slot = lax.broadcasted_iota(jnp.int32, (depth, tokens), 0).astype(F32)
    picks = [
        jnp.where(jnp.broadcast_to(rank[i : i + 1], slot.shape) == slot, 1.0, 0.0)
        for i in range(len(experts))
    ]
    return picks, weights


def routes_of(pack_ref, tokens):
    meta = pack_ref[tokens : tokens + META, 0:tokens].astype(F32)
    return meta[0:8], meta[8:16]


def select_kernel(plane, depth, at_ref, pack_ref, *rest):
    outs, scratch = rest[-plane - 1 : -1], rest[-1]
    tokens = pack_ref.shape[0] - META
    ids, probs = routes_of(pack_ref, tokens)
    experts = [at_ref[0] * plane + (at_ref[1] ^ o) for o in range(plane)]
    picks, weights = slot_tables(ids, probs, experts, depth, scratch)
    weighted = jnp.concatenate([p * w for p, w in zip(picks, weights)], 0).astype(BF16)
    rows = dot(weighted, pack_ref[0:tokens, :])
    for o in range(plane):
        outs[o][...] = rows[o * depth : (o + 1) * depth].astype(BF16)


def factor_kernel(at_ref, x_ref, gate_own, gate_other, up_own, up_other, out_ref):
    width = gate_own.shape[0]
    core = at_ref[2]
    own = x_ref[:, pl.ds(pl.multiple_of(core * width, 128), width)]
    other = x_ref[:, pl.ds(pl.multiple_of((1 - core) * width, 128), width)]
    gate = dot(own, gate_own[...]) + dot(other, gate_other[...])
    up = dot(own, up_own[...]) + dot(other, up_other[...])
    sig = 1.0 / (1.0 + jnp.exp(-gate))
    silu = gate * sig
    out_ref[0] = (silu * up).astype(BF16)
    out_ref[1] = (up * sig * (1.0 + gate * (1.0 - sig))).astype(BF16)
    out_ref[2] = silu.astype(BF16)


def raw_kernel(plane, *refs):
    parts, down_ref = refs[:plane], refs[plane]
    rows_ref, full_ref, half_ref = refs[-3:]
    rows = stacked([part[...] for part in parts])
    rows_ref[...] = rows
    raw = dot(rows, down_ref[...])
    full_ref[...] = raw
    half_ref[...] = raw.astype(BF16)


def middle_kernel(r, plane, depth, at_ref, own_ref, other_ref, mine_ref, theirs_ref, gate_ref, up_ref, *rest):
    outs, gates_ref = rest[-plane - 4 : -4], rest[-4]
    held, grads, sem = rest[-3:]

    @pl.when(pl.program_id(0) == 0)
    def _():
        layer = at_ref[0] ^ r
        half, place = layer // (LAYERS // 2), layer % (LAYERS // 2)

        @pl.when(half == at_ref[2])
        def _():
            copy = pltpu.make_async_copy(mine_ref.at[:, place], held, sem)
            copy.start()
            copy.wait()

        @pl.when(half != at_ref[2])
        def _():
            copy = pltpu.make_async_copy(theirs_ref.at[:, place], held, sem)
            copy.start()
            copy.wait()

        raw = own_ref[...] + other_ref[...].astype(F32)
        spots = [at_ref[1] ^ o for o in range(plane)]
        hidden, to_gate, to_up = [
            jnp.concatenate([held[k, spot].astype(F32) for spot in spots], 0) for k in range(3)
        ]
        ones = jnp.ones((8, raw.shape[1]), F32)
        gates_ref[...] = lax.dot_general(
            ones, raw * hidden, COLS_COLS, precision=lax.Precision.HIGHEST, preferred_element_type=F32
        )
        grads[0] = (raw * to_gate).astype(BF16)
        grads[1] = (raw * to_up).astype(BF16)

    rows = dot(grads[0], gate_ref[...], COLS_COLS) + dot(grads[1], up_ref[...], COLS_COLS)
    for o in range(plane):
        outs[o][...] = rows[o * depth : (o + 1) * depth].astype(BF16)


def home_sum(plane, depth, at_ref, pack_ref, back, scratch):
    tokens = pack_ref.shape[0] - META
    ids, probs = routes_of(pack_ref, tokens)
    experts = [at_ref[0] * plane + (at_ref[1] ^ o) for o in range(plane)]
    picks, _ = slot_tables(ids, probs, experts, depth, scratch)
    picked = jnp.concatenate(picks, 0).astype(BF16)
    return dot(picked, stacked([ref[...] for ref in back]), ROWS_ROWS)


def home_kernel(plane, depth, at_ref, pack_ref, *rest):
    back, out_ref, scratch = rest[:plane], rest[-2], rest[-1]
    out_ref[...] = home_sum(plane, depth, at_ref, pack_ref, back, scratch).astype(BF16)


def final_kernel(plane, depth, at_ref, pack_ref, *rest):
    back, far, out_ref, scratch = rest[:plane], rest[plane : plane + 3], rest[-2], rest[-1]
    total = home_sum(plane, depth, at_ref, pack_ref, back, scratch)
    for ref in far:
        total = total + ref[...].astype(F32)
    out_ref[...] = total.astype(BF16)


def router_kernel(plane, depth, at_ref, pack_ref, *rest):
    sums, out_ref, scratch = rest[:LAYERS], rest[-2], rest[-1]
    tokens = pack_ref.shape[0] - META
    top = out_ref.shape[1]
    ids, probs = routes_of(pack_ref, tokens)
    experts = [
        (at_ref[0] ^ r) * plane + (at_ref[1] ^ o) for r in range(LAYERS) for o in range(plane)
    ]
    picks, _ = slot_tables(ids, probs, experts, depth, scratch)
    total = jnp.zeros((8, tokens), F32)
    for r in range(LAYERS):
        for o in range(plane):
            got = sums[r][o, r * 8 : r * 8 + 8, o * depth : (o + 1) * depth]
            i = r * plane + o
            routed = lax.dot_general(
                got, picks[i], (((1,), (0,)), ((), ())),
                precision=lax.Precision.HIGHEST, preferred_element_type=F32,
            )
            total = total + jnp.where(ids == experts[i].astype(F32), routed, 0.0)
    ratio = (total / jnp.where(probs > 0.0, probs, 1.0)).astype(BF16)
    eye = (
        lax.broadcasted_iota(jnp.int32, (8, top), 0) == lax.broadcasted_iota(jnp.int32, (8, top), 1)
    ).astype(BF16)
    out_ref[...] = dot(ratio, eye, ROWS_ROWS).astype(BF16)


def down_kernel(plane, at_ref, *refs):
    rows = refs[:LAYERS]
    mine_ref, theirs_ref, out_ref, held, hidden, sem = refs[-6:]
    size = rows[0].shape[0]

    @pl.when(pl.program_id(0) == 0)
    def _():
        half = LAYERS // 2
        copies = [
            pltpu.make_async_copy(mine_ref.at[0], held.at[pl.ds(at_ref[2] * half, half)], sem.at[0]),
            pltpu.make_async_copy(theirs_ref.at[0], held.at[pl.ds((1 - at_ref[2]) * half, half)], sem.at[1]),
        ]
        for copy in copies:
            copy.start()
        for copy in copies:
            copy.wait()
        for r in range(LAYERS):
            hidden[r * size : (r + 1) * size, :] = stacked(
                [held[at_ref[0] ^ r, at_ref[1] ^ o] for o in range(plane)]
            )

    out_ref[...] = dot(jnp.concatenate([ref[...] for ref in rows], 0), hidden[...], ROWS_ROWS)


def body(out_grad, expert_ids, gate_probs, saved_inputs, gate_weight, up_weight, down_weight):
    tokens, width = out_grad.shape
    top = expert_ids.shape[1]
    experts = lax.axis_size("expert")
    plane = experts // LAYERS
    local_rows = saved_inputs.shape[1]
    slots = local_rows * lax.axis_size("fsdp")
    depth = slots // experts
    units = gate_weight.shape[2]
    group = plane * depth
    me = lax.axis_index("expert")
    at = jnp.stack([me // plane, me % plane, lax.axis_index("fsdp")]).astype(jnp.int32)
    gate_own, up_own, down_own = gate_weight[0], up_weight[0], down_weight[0]

    def other_core(array):
        return lax.ppermute(array, "fsdp", [(0, 1), (1, 0)])

    def other_layer(array, r):
        return lax.ppermute(array, "expert", [(e, e ^ (r * plane)) for e in range(experts)])

    def to_plane(rows):
        return [rows[0]] + [
            lax.ppermute(rows[o], "expert", [(e, e ^ o) for e in range(experts)])
            for o in range(1, plane)
        ]

    shape = jax.ShapeDtypeStruct
    scratch = pltpu.VMEM((max(8, plane), tokens), F32)
    pack = pl.pallas_call(
        pack_kernel, out_shape=shape((tokens + META, width), BF16), in_specs=[VMEM] * 3, out_specs=VMEM
    )(expert_ids, gate_probs, out_grad)

    def select(block, deps):
        return pl.pallas_call(
            functools.partial(select_kernel, plane, depth),
            out_shape=[shape((depth, width), BF16)] * plane,
            in_specs=[SMEM, VMEM] + [ANY] * len(deps),
            out_specs=[VMEM] * plane,
            scratch_shapes=[scratch],
            compiler_params=params(),
            cost_estimate=pl.CostEstimate(flops=2 * group * tokens * width, bytes_accessed=4 * group * width, transcendentals=0),
        )(at, block, *deps)

    def raw_sum(parts, deps):
        return pl.pallas_call(
            functools.partial(raw_kernel, plane),
            out_shape=[shape((group, width), BF16), shape((group, units), F32), shape((group, units), BF16)],
            in_specs=[VMEM] * (plane + 1) + [ANY] * len(deps),
            out_specs=[VMEM] * 3,
            compiler_params=params(),
            cost_estimate=pl.CostEstimate(flops=2 * group * units * width, bytes_accessed=4 * width * units, transcendentals=0),
        )(*parts, down_own, *deps)

    def middle(r, own, other, mine, theirs, deps):
        tile = TILE
        return pl.pallas_call(
            functools.partial(middle_kernel, r, plane, depth),
            out_shape=[shape((depth, width), BF16)] * plane + [shape((8, group), F32)],
            grid=(width // tile,),
            in_specs=[
                SMEM,
                pl.BlockSpec((group, units), lambda j: (0, 0)),
                pl.BlockSpec((group, units), lambda j: (0, 0)),
                ANY,
                ANY,
                pl.BlockSpec((tile, units), lambda j: (j, 0)),
                pl.BlockSpec((tile, units), lambda j: (j, 0)),
            ]
            + [ANY] * len(deps),
            out_specs=[pl.BlockSpec((depth, tile), lambda j: (0, j))] * plane
            + [pl.BlockSpec((8, group), lambda j: (0, 0))],
            scratch_shapes=[
                pltpu.VMEM((3, plane, depth, units), BF16),
                pltpu.VMEM((2, group, units), BF16),
                pltpu.SemaphoreType.DMA,
            ],
            compiler_params=params(),
            cost_estimate=pl.CostEstimate(flops=4 * group * units * width, bytes_accessed=8 * width * units, transcendentals=0),
        )(at, own, other, mine, theirs, gate_own, up_own, *deps)

    def home(block, back, deps):
        return pl.pallas_call(
            functools.partial(home_kernel, plane, depth),
            out_shape=shape((tokens, width), BF16),
            in_specs=[SMEM] + [VMEM] * (plane + 1) + [ANY] * len(deps),
            out_specs=VMEM,
            scratch_shapes=[scratch],
            compiler_params=params(),
            cost_estimate=pl.CostEstimate(flops=2 * group * tokens * width, bytes_accessed=4 * group * width, transcendentals=0),
        )(at, block, *back, *deps)

    blocks = [pack, other_layer(pack, 1), None, None]
    gate_other = other_core(gate_own)
    up_other = other_core(up_own)
    sent = [select(pack, ()), None, None, None]
    arrived = [to_plane(sent[0]), None, None, None]
    blocks[2] = other_layer(pack, 2)
    sent[1] = select(blocks[1], sent[0][:1])
    arrived[1] = to_plane(sent[1])
    blocks[3] = other_layer(pack, 3)

    factors = pl.pallas_call(
        factor_kernel,
        out_shape=shape((3, local_rows, units), BF16),
        grid=(units // TILE,),
        in_specs=[SMEM, pl.BlockSpec((local_rows, 2 * width), lambda j: (0, 0))]
        + [pl.BlockSpec((width, TILE), lambda j: (0, j))] * 4
        + [],
        out_specs=pl.BlockSpec((3, local_rows, TILE), lambda j: (0, 0, j)),
        compiler_params=params(40),
        cost_estimate=pl.CostEstimate(flops=8 * local_rows * units * width, bytes_accessed=16 * width * units, transcendentals=local_rows * units),
    )(at, saved_inputs[0], gate_own, gate_other, up_own, up_other)
    mine = factors.reshape(3, LAYERS // 2, plane, depth, units)
    theirs = other_core(factors).reshape(3, LAYERS // 2, plane, depth, units)

    sent[2] = select(blocks[2], (factors, sent[1][0]))
    arrived[2] = to_plane(sent[2])
    raws = [None] * LAYERS
    raws[0] = raw_sum(arrived[0], sent[2][:1])
    swaps = [other_core(raws[0][2]), None, None, None]
    raws[1] = raw_sum(arrived[1], raws[0][1:2])
    swaps[1] = other_core(raws[1][2])
    sent[3] = select(blocks[3], raws[1][1:2])
    arrived[3] = to_plane(sent[3])
    slot_rows = [None] * LAYERS
    slot_rows[0] = middle(0, raws[0][1], swaps[0], mine, theirs, sent[3][:1])
    slot_rows[1] = middle(1, raws[1][1], swaps[1], mine, theirs, slot_rows[0][-1:])
    raws[2] = raw_sum(arrived[2], slot_rows[1][-1:])
    swaps[2] = other_core(raws[2][2])
    slot_rows[2] = middle(2, raws[2][1], swaps[2], mine, theirs, ())
    back = [None] * LAYERS
    back[2] = to_plane(slot_rows[2][:plane])
    raws[3] = raw_sum(arrived[3], slot_rows[2][-1:])
    swaps[3] = other_core(raws[3][2])
    slot_rows[3] = middle(3, raws[3][1], swaps[3], mine, theirs, ())
    back[3] = to_plane(slot_rows[3][:plane])
    back[1] = to_plane(slot_rows[1][:plane])
    back[0] = to_plane(slot_rows[0][:plane])

    gates = jnp.concatenate([slot_rows[r][-1] for r in range(LAYERS)])
    gates = jnp.stack(to_plane([gates] * plane))
    far_gates = [gates] + [other_layer(gates, r) for r in range(1, LAYERS)]

    tile = TILE
    down_grad = pl.pallas_call(
        functools.partial(down_kernel, plane),
        out_shape=shape((width, units), F32),
        grid=(width // tile,),
        in_specs=[SMEM]
        + [pl.BlockSpec((group, tile), lambda j: (0, j))] * LAYERS
        + [ANY] * 3,
        out_specs=pl.BlockSpec((tile, units), lambda j: (j, 0)),
        scratch_shapes=[
            pltpu.VMEM((LAYERS, plane, depth, units), BF16),
            pltpu.VMEM((slots, units), BF16),
            pltpu.SemaphoreType.DMA((2,)),
        ],
        compiler_params=params(),
        cost_estimate=pl.CostEstimate(flops=2 * slots * units * width, bytes_accessed=8 * width * units, transcendentals=0),
    )(at, *[raws[r][0] for r in range(LAYERS)], slot_rows[3][-1], mine, theirs)

    far = [None] * LAYERS
    sums = home(blocks[2], back[2], (slot_rows[3][-1],))
    far[2] = other_layer(sums, 2)
    sums = home(blocks[3], back[3], (sums,))
    far[3] = other_layer(sums, 3)
    sums = home(blocks[1], back[1], (sums,))
    far[1] = other_layer(sums, 1)

    gate_grad = pl.pallas_call(
        functools.partial(router_kernel, plane, depth),
        out_shape=shape((tokens, top), BF16),
        in_specs=[SMEM, VMEM] + [VMEM] * LAYERS + [ANY],
        out_specs=VMEM,
        scratch_shapes=[pltpu.VMEM((experts, tokens), F32)],
        compiler_params=params(),
    )(at, pack, *far_gates, sums)
    input_grad = pl.pallas_call(
        functools.partial(final_kernel, plane, depth),
        out_shape=shape((tokens, width), BF16),
        in_specs=[SMEM] + [VMEM] * (plane + 4) + [ANY],
        out_specs=VMEM,
        scratch_shapes=[scratch],
        compiler_params=params(),
    )(at, pack, *back[0], far[1], far[2], far[3], gate_grad)
    return input_grad, gate_grad, down_grad[None]


def solution(mesh):
    return jax.shard_map(
        body,
        mesh=mesh,
        in_specs=(
            P("expert", "fsdp"),
            P("expert", None),
            P("expert", None),
            P("expert", "fsdp", None),
            P("expert", "fsdp", None),
            P("expert", "fsdp", None),
            P("expert", "fsdp", None),
        ),
        out_specs=(P("expert", "fsdp"), P("expert", None), P("expert", "fsdp", None)),
        check_vma=False,
    )
```

```python
import functools
import jax
import jax.numpy as jnp
from jax import lax
from jax.experimental import pallas as pl
from jax.experimental.pallas import tpu as pltpu
from jax.sharding import PartitionSpec as P

LAYERS = 4
META = 16
EXTRA = 8
TILE = 256
COST = 2 * 10**10
CHAIN = "factor0 select1 factor1 factor2 raw0 select2 middle0 raw1 select3 middle1 raw2".split()
BF16, F32 = jnp.bfloat16, jnp.float32
ROWS_ROWS = (((0,), (0,)), ((), ()))
COLS_COLS = (((1,), (1,)), ((), ()))
VMEM = pl.BlockSpec(memory_space=pltpu.VMEM)
SMEM = pl.BlockSpec(memory_space=pltpu.SMEM)
ANY = pl.BlockSpec(memory_space=pl.ANY)


def dot(a, b, dims=(((1,), (0,)), ((), ()))):
    return lax.dot_general(a, b, dims, preferred_element_type=F32)


def stacked(refs):
    return jnp.concatenate([ref.astype(F32) for ref in refs], 0).astype(BF16)


def params(mib=24):
    return pltpu.CompilerParams(vmem_limit_bytes=mib * 1024 * 1024)


def pack_kernel(ids_ref, probs_ref, tok_ref, out_ref):
    top, tokens = ids_ref.shape
    width = tok_ref.shape[1]
    none = jnp.full((8 - top, tokens), -1.0, F32)
    meta = jnp.concatenate([ids_ref[...].astype(F32), none, probs_ref[...], none], 0).astype(BF16)
    out_ref[0:tokens, :] = tok_ref[...]
    out_ref[tokens : tokens + META, :] = jnp.zeros((META, width), BF16)
    out_ref[tokens : tokens + META, 0:tokens] = meta


def slot_tables(ids, probs, experts, depth, scratch):
    tokens = ids.shape[1]
    scratch[...] = jnp.zeros_like(scratch)
    weights = []
    for i, expert in enumerate(experts):
        hit = ids == expert.astype(F32)
        scratch[i : i + 1, :] = jnp.max(jnp.where(hit, 1.0, 0.0), axis=0, keepdims=True)
        weights.append(jnp.sum(jnp.where(hit, probs, 0.0), axis=0, keepdims=True))
    before = (
        lax.broadcasted_iota(jnp.int32, (tokens, tokens), 0)
        < lax.broadcasted_iota(jnp.int32, (tokens, tokens), 1)
    ).astype(BF16)
    member = scratch[...]
    rank = jnp.where(member > 0.5, dot(member.astype(BF16), before), -1.0)
    slot = lax.broadcasted_iota(jnp.int32, (depth, tokens), 0).astype(F32)
    picks = [
        jnp.where(jnp.broadcast_to(rank[i : i + 1], slot.shape) == slot, 1.0, 0.0)
        for i in range(len(experts))
    ]
    return picks, weights


def routes_of(meta_ref):
    meta = meta_ref[...].astype(F32)
    return meta[0:8], meta[8:16]


def select_kernel(plane, depth, at_ref, pack_ref, own_ref, *rest):
    *outs, meta_ref, relay_ref, scratch = rest[-plane - 3 :]
    tokens = pack_ref.shape[0] - META
    relay_ref[...] = own_ref[0 : relay_ref.shape[0], :]
    meta_ref[...] = pack_ref[tokens : tokens + META, 0:tokens]
    ids, probs = routes_of(meta_ref)
    experts = [at_ref[0] * plane + (at_ref[1] ^ o) for o in range(plane)]
    picks, weights = slot_tables(ids, probs, experts, depth, scratch)
    weighted = jnp.concatenate([p * w for p, w in zip(picks, weights)], 0).astype(BF16)
    rows = dot(weighted, pack_ref[0:tokens, :])
    for o in range(plane):
        outs[o][...] = rows[o * depth : (o + 1) * depth].astype(BF16)


def factor_kernel(at_ref, x_ref, gate_own, gate_other, up_own, up_other, *rest):
    out_ref = rest[-1]
    width = gate_own.shape[0]
    core = at_ref[2]
    own = x_ref[:, pl.ds(pl.multiple_of(core * width, 128), width)]
    other = x_ref[:, pl.ds(pl.multiple_of((1 - core) * width, 128), width)]
    gate = dot(own, gate_own[...]) + dot(other, gate_other[...])
    up = dot(own, up_own[...]) + dot(other, up_other[...])
    sig = 1.0 / (1.0 + jnp.exp(-gate))
    silu = gate * sig
    out_ref[0] = (silu * up).astype(BF16)
    out_ref[1] = (up * sig * (1.0 + gate * (1.0 - sig))).astype(BF16)
    out_ref[2] = silu.astype(BF16)


def raw_kernel(plane, *refs):
    parts, down_ref = refs[:plane], refs[plane]
    rows_ref, full_ref, half_ref = refs[-3:]
    rows = stacked([part[...] for part in parts])
    rows_ref[...] = rows
    raw = dot(rows, down_ref[...])
    full_ref[...] = raw
    half_ref[...] = raw.astype(BF16)


def middle_kernel(r, plane, depth, at_ref, own_ref, other_ref, mine_ref, theirs_ref, gate_ref, up_ref, *rest):
    *outs, held, sem = rest[-plane - 2 :]
    width = gate_ref.shape[0]
    layer = at_ref[0] ^ r
    half, place = layer // (LAYERS // 2), layer % (LAYERS // 2)

    @pl.when(half == at_ref[2])
    def _():
        pltpu.make_async_copy(mine_ref.at[:, place], held, sem).start()

    @pl.when(half != at_ref[2])
    def _():
        pltpu.make_async_copy(theirs_ref.at[:, place], held, sem).start()

    raw = own_ref[...] + other_ref[...].astype(F32)
    pltpu.make_async_copy(mine_ref.at[:, place], held, sem).wait()
    spots = [at_ref[1] ^ o for o in range(plane)]
    hidden, to_gate, to_up = [
        jnp.concatenate([held[k, spot].astype(F32) for spot in spots], 0) for k in range(3)
    ]
    gate_grad = (raw * to_gate).astype(BF16)
    up_grad = (raw * to_up).astype(BF16)
    for j in range(0, width, TILE):
        cols = slice(j, j + TILE)
        rows = dot(gate_grad, gate_ref[cols, :], COLS_COLS) + dot(up_grad, up_ref[cols, :], COLS_COLS)
        for o in range(plane):
            outs[o][0:depth, cols] = rows[o * depth : (o + 1) * depth].astype(BF16)
    shares = raw * hidden
    lanes = shares[:, 0:128]
    for j in range(128, shares.shape[1], 128):
        lanes = lanes + shares[:, j : j + 128]
    ones = jnp.ones((EXTRA, 128), F32)
    for o in range(plane):
        outs[o][depth : depth + EXTRA, 0:depth] = lax.dot_general(
            ones, lanes[o * depth : (o + 1) * depth], COLS_COLS,
            precision=lax.Precision.HIGHEST, preferred_element_type=F32,
        ).astype(BF16)


def home_sum(plane, depth, at_ref, meta_ref, back, scratch):
    ids, probs = routes_of(meta_ref)
    experts = [at_ref[0] * plane + (at_ref[1] ^ o) for o in range(plane)]
    picks, _ = slot_tables(ids, probs, experts, depth, scratch)
    picks = [pick.astype(BF16) for pick in picks]
    picked = jnp.concatenate([pick.astype(F32) for pick in picks], 0).astype(BF16)
    total = dot(picked, stacked([ref[0:depth, :] for ref in back]), ROWS_ROWS)
    routed = jnp.zeros(ids.shape, F32)
    for ref, expert, pick in zip(back, experts, picks):
        mine = dot(ref[depth : depth + EXTRA, 0:depth], pick)
        routed = routed + jnp.where(ids == expert.astype(F32), mine, 0.0)
    return total, routed, probs


def home_kernel(plane, depth, passed, at_ref, meta_ref, *rest):
    back, out_ref, scratch = rest[:plane], rest[-2 - passed], rest[-1]
    tokens = meta_ref.shape[1]
    total, routed, _ = home_sum(plane, depth, at_ref, meta_ref, back, scratch)
    out_ref[0:tokens, :] = total.astype(BF16)
    out_ref[tokens : tokens + META, 0:tokens] = jnp.concatenate([routed, routed], 0).astype(BF16)


def own_kernel(plane, depth, at_ref, meta_ref, *rest):
    back, (out_ref, routed_ref, scratch) = rest[:plane], rest[-3:]
    out_ref[...], routed_ref[...], _ = home_sum(plane, depth, at_ref, meta_ref, back, scratch)


def final_kernel(meta_ref, own_ref, routed_ref, *rest):
    far, (grad_ref, router_ref) = rest[:3], rest[-2:]
    tokens = meta_ref.shape[1]
    _, probs = routes_of(meta_ref)
    total, routed = own_ref[...], routed_ref[...]
    for ref in far:
        total = total + ref[0:tokens, :].astype(F32)
        routed = routed + ref[tokens : tokens + META, 0:tokens].astype(F32)[0 : routed.shape[0]]
    grad_ref[...] = total.astype(BF16)
    ratio = routed / jnp.where(probs > 0.0, probs, 1.0)
    router_ref[...] = ratio[0 : router_ref.shape[0]].astype(BF16)


def down_kernel(plane, at_ref, *refs):
    rows = refs[:LAYERS]
    mine_ref, theirs_ref = refs[LAYERS : LAYERS + 2]
    out_ref, held, hidden, sem = refs[-4:]
    size = rows[0].shape[0]

    @pl.when(pl.program_id(0) == 0)
    def _():
        half = LAYERS // 2
        copies = [
            pltpu.make_async_copy(mine_ref.at[0], held.at[pl.ds(at_ref[2] * half, half)], sem.at[0]),
            pltpu.make_async_copy(theirs_ref.at[0], held.at[pl.ds((1 - at_ref[2]) * half, half)], sem.at[1]),
        ]
        for copy in copies:
            copy.start()
        for copy in copies:
            copy.wait()
        for r in range(LAYERS):
            hidden[r * size : (r + 1) * size, :] = stacked(
                [held[at_ref[0] ^ r, at_ref[1] ^ o] for o in range(plane)]
            )

    out_ref[...] = dot(jnp.concatenate([ref[...] for ref in rows], 0), hidden[...], ROWS_ROWS)


def body(out_grad, expert_ids, gate_probs, saved_inputs, gate_weight, up_weight, down_weight):
    tokens, width = out_grad.shape
    top = expert_ids.shape[1]
    experts = lax.axis_size("expert")
    plane = experts // LAYERS
    local_rows = saved_inputs.shape[1]
    slots = local_rows * lax.axis_size("fsdp")
    depth = slots // experts
    units = gate_weight.shape[2]
    group = plane * depth
    me = lax.axis_index("expert")
    at = jnp.stack([me // plane, me % plane, lax.axis_index("fsdp")]).astype(jnp.int32)
    gate_own, up_own, down_own = gate_weight[0], up_weight[0], down_weight[0]

    def other_core(array):
        return lax.ppermute(array, "fsdp", [(0, 1), (1, 0)])

    def swapped(array, mask):
        return lax.ppermute(array, "expert", [(e, e ^ mask) for e in range(experts)])

    def other_layer(array, r):
        return swapped(array, r * plane)

    def to_plane(rows):
        return [rows[0]] + [swapped(rows[o], o) for o in range(1, plane)]

    def call(name, kernel, outs, ins, in_specs, out_specs, scratch=(), deps=(), through=(), mib=24, grid=()):
        extra = list(deps) + list(through)
        first = len(ins) + len(deps)
        return pl.pallas_call(
            kernel,
            name=name,
            out_shape=list(outs) + [shape(a.shape, a.dtype) for a in through],
            grid=grid,
            in_specs=list(in_specs) + [ANY] * len(extra),
            out_specs=list(out_specs) + [ANY] * len(through),
            scratch_shapes=list(scratch),
            input_output_aliases={first + i: len(outs) + i for i in range(len(through))},
            compiler_params=params(mib),
            cost_estimate=pl.CostEstimate(flops=COST, bytes_accessed=0, transcendentals=0),
        )(*ins, *extra)

    shape = jax.ShapeDtypeStruct
    table = pltpu.VMEM((max(8, plane), tokens), F32)
    slab = shape((depth, width), BF16)
    longer = shape((depth + EXTRA, width), BF16)
    (pack,) = call(
        "pack",
        pack_kernel,
        [shape((tokens + META, width), BF16)],
        [expert_ids.T, gate_probs.T, out_grad],
        [VMEM] * 3,
        [VMEM],
    )

    def select(block, deps, relay=False):
        outs = call(
            "select",
            functools.partial(select_kernel, plane, depth),
            [slab] * plane + [shape((META, tokens), BF16), shape(pack.shape if relay else (META, width), BF16)],
            [at, block, pack],
            [SMEM, VMEM, VMEM],
            [VMEM] * (plane + 2),
            [table],
            deps,
        )
        return outs[:plane], outs[plane], outs[plane + 1]

    def raw_sum(parts, deps):
        rows, full, half = call(
            "raw",
            functools.partial(raw_kernel, plane),
            [shape((group, width), BF16), shape((group, units), F32), shape((group, units), BF16)],
            [*parts, down_own],
            [VMEM] * (plane + 1),
            [VMEM] * 3,
            deps=deps,
        )
        return rows, full, other_core(half)

    def middle(r, raw, deps):
        return call(
            "middle",
            functools.partial(middle_kernel, r, plane, depth),
            [longer] * plane,
            [at, raw[1], raw[2], mine, theirs, gate_own, up_own],
            [SMEM, VMEM, VMEM, ANY, ANY, VMEM, VMEM],
            [VMEM] * plane,
            [pltpu.VMEM((3, plane, depth, units), BF16), pltpu.SemaphoreType.DMA],
            deps,
        )

    def home(r, back, deps, through=()):
        out, *passed = call(
            "home",
            functools.partial(home_kernel, plane, depth, len(through)),
            [shape((tokens + META, width), BF16)],
            [at, metas[r], *back],
            [SMEM, VMEM] + [VMEM] * plane,
            [VMEM],
            [table],
            deps,
            through,
        )
        return out, passed

    blocks = [pack, other_layer(pack, 1), None, None]
    gate_other, up_other = other_core(gate_own), other_core(up_own)
    metas = [None] * LAYERS
    rows, metas[0], relay = select(pack, (), True)
    arrived = [to_plane(rows), None, None, None]
    blocks[2] = other_layer(relay, 2)
    factors = []

    def factor(dep):
        j = len(factors)
        whole, part = (lambda i: (0, 0)), (lambda i: (0, j))
        (out,) = pl.pallas_call(
            factor_kernel,
            name="factor",
            out_shape=[shape((3, local_rows, units), BF16)],
            grid=(1,),
            in_specs=[SMEM, pl.BlockSpec((local_rows, 2 * width), whole)]
            + [pl.BlockSpec((width, TILE), part)] * 4
            + [ANY] * (1 + min(j, 1)),
            out_specs=[pl.BlockSpec((3, local_rows, TILE), lambda i: (0, 0, j))],
            input_output_aliases={7: 0} if j else {},
            compiler_params=params(32),
            cost_estimate=pl.CostEstimate(flops=COST, bytes_accessed=0, transcendentals=0),
        )(at, saved_inputs[0], gate_own, gate_other, up_own, up_other, dep, *factors[-1:])
        factors.append(out)
        return out

    raws, slot_rows = [None] * LAYERS, [None] * LAYERS
    last = rows[0]
    for step in CHAIN:
        kind, r = step[:-1], int(step[-1])
        if kind == "factor":
            last = factor(last)
            if len(factors) == units // TILE:
                view = (3, LAYERS // 2, plane, depth, units)
                mine, theirs = last.reshape(view), other_core(last).reshape(view)
        elif kind == "select":
            rows, metas[r], relay = select(blocks[r], [last], r == 1)
            arrived[r] = to_plane(rows)
            if r == 1:
                blocks[3] = other_layer(relay, 3)
            last = rows[0]
        elif kind == "raw":
            raws[r] = raw_sum(arrived[r], [last])
            last = raws[r][1]
        else:
            slot_rows[r] = middle(r, raws[r], [last])
            last = slot_rows[r][0]

    back, far = [None] * LAYERS, [None] * LAYERS
    slot_rows[2] = middle(2, raws[2], [last])
    back[2] = to_plane(slot_rows[2])
    raws[3] = raw_sum(arrived[3], slot_rows[2][:1])
    slot_rows[3] = middle(3, raws[3], ())
    back[3] = to_plane(slot_rows[3])
    sums, passed = home(2, back[2], slot_rows[3][:1], slot_rows[1])
    far[2] = other_layer(sums, 2)
    back[1] = to_plane(passed)
    sums, passed = home(3, back[3], [sums], slot_rows[0])
    far[3] = other_layer(sums, 3)
    back[0] = to_plane(passed)
    (down_grad,) = call(
        "down",
        functools.partial(down_kernel, plane),
        [shape((width, units), F32)],
        [at, *[raws[r][0] for r in range(LAYERS)], mine, theirs],
        [SMEM] + [pl.BlockSpec((group, TILE), lambda j: (0, j))] * LAYERS + [ANY, ANY],
        [pl.BlockSpec((TILE, units), lambda j: (j, 0))],
        [
            pltpu.VMEM((LAYERS, plane, depth, units), BF16),
            pltpu.VMEM((slots, units), BF16),
            pltpu.SemaphoreType.DMA((2,)),
        ],
        [sums],
        grid=(width // TILE,),
    )
    sums, _ = home(1, back[1], [down_grad])
    far[1] = other_layer(sums, 1)
    own = call(
        "own",
        functools.partial(own_kernel, plane, depth),
        [shape((tokens, width), F32), shape((8, tokens), F32)],
        [at, metas[0], *back[0]],
        [SMEM] + [VMEM] * (plane + 1),
        [VMEM] * 2,
        [table],
        [sums],
    )
    input_grad, router = call(
        "final",
        final_kernel,
        [shape((tokens, width), BF16), shape((top, tokens), BF16)],
        [metas[0], *own, far[1], far[2], far[3]],
        [VMEM] * 6,
        [VMEM] * 2,
    )
    return input_grad, router.T, down_grad[None]


def solution(mesh):
    return jax.shard_map(
        body,
        mesh=mesh,
        in_specs=(
            P("expert", "fsdp"),
            P("expert", None),
            P("expert", None),
            P("expert", "fsdp", None),
            P("expert", "fsdp", None),
            P("expert", "fsdp", None),
            P("expert", "fsdp", None),
        ),
        out_specs=(P("expert", "fsdp"), P("expert", None), P("expert", "fsdp", None)),
        check_vma=False,
    )
```

```python
import functools
import jax
import jax.numpy as jnp
from jax import lax
from jax.experimental import pallas as pl
from jax.experimental.pallas import tpu as pltpu
from jax.sharding import PartitionSpec as P

LAYERS = 4
META = 16
EXTRA = 8
TILE = 256
COST = 20000000000
CHAIN = (
    ("factor", 0),
    ("factor", 1),
    ("factor", 2),
    ("select", 1, 0),
    ("select", 2),
    ("raw", (2,)),
    ("select", 3, 1),
    ("middle", 2),
    ("raw", (0, 1)),
    ("raw", (3,)),
    ("middle", 3),
    ("home", 2),
    ("middle", 1),
    ("home", 3),
    ("middle", 0),
    ("down", 0),
    ("home", 1),
)
BF16, F32 = jnp.bfloat16, jnp.float32
ROWS_ROWS = (((0,), (0,)), ((), ()))
COLS_COLS = (((1,), (1,)), ((), ()))
VMEM = pl.BlockSpec(memory_space=pltpu.VMEM)
SMEM = pl.BlockSpec(memory_space=pltpu.SMEM)
ANY = pl.BlockSpec(memory_space=pl.ANY)


def dot(a, b, dims=(((1,), (0,)), ((), ()))):
    return lax.dot_general(a, b, dims, preferred_element_type=F32)


def stacked(refs):
    return jnp.concatenate([ref.astype(F32) for ref in refs], 0).astype(BF16)


def params(mib=24):
    return pltpu.CompilerParams(vmem_limit_bytes=mib * 1024 * 1024)


def pack_kernel(ids_ref, probs_ref, tok_ref, out_ref):
    top, tokens = ids_ref.shape
    width = tok_ref.shape[1]
    none = jnp.full((8 - top, tokens), -1.0, F32)
    meta = jnp.concatenate([ids_ref[...].astype(F32), none, probs_ref[...], none], 0).astype(BF16)
    out_ref[0:tokens, :] = tok_ref[...]
    out_ref[tokens : tokens + META, :] = jnp.zeros((META, width), BF16)
    out_ref[tokens : tokens + META, 0:tokens] = meta


def slot_tables(ids, probs, experts, depth, scratch):
    tokens = ids.shape[1]
    scratch[...] = jnp.zeros_like(scratch)
    weights = []
    for i, expert in enumerate(experts):
        hit = ids == expert.astype(F32)
        scratch[i : i + 1, :] = jnp.max(jnp.where(hit, 1.0, 0.0), axis=0, keepdims=True)
        weights.append(jnp.sum(jnp.where(hit, probs, 0.0), axis=0, keepdims=True))
    before = (
        lax.broadcasted_iota(jnp.int32, (tokens, tokens), 0)
        < lax.broadcasted_iota(jnp.int32, (tokens, tokens), 1)
    ).astype(BF16)
    member = scratch[...]
    rank = jnp.where(member > 0.5, dot(member.astype(BF16), before), -1.0)
    slot = lax.broadcasted_iota(jnp.int32, (depth, tokens), 0).astype(F32)
    picks = [
        jnp.where(jnp.broadcast_to(rank[i : i + 1], slot.shape) == slot, 1.0, 0.0)
        for i in range(len(experts))
    ]
    return picks, weights


def routes_of(meta_ref):
    meta = meta_ref[...].astype(F32)
    return meta[0:8], meta[8:16]


def select_kernel(plane, depth, at_ref, pack_ref, *rest):
    *outs, meta_ref, scratch = rest[-plane - 2 :]
    tokens = pack_ref.shape[0] - META
    meta_ref[...] = pack_ref[tokens : tokens + META, 0:tokens]
    ids, probs = routes_of(meta_ref)
    experts = [at_ref[0] * plane + (at_ref[1] ^ o) for o in range(plane)]
    picks, weights = slot_tables(ids, probs, experts, depth, scratch)
    weighted = jnp.concatenate([p * w for p, w in zip(picks, weights)], 0).astype(BF16)
    rows = dot(weighted, pack_ref[0:tokens, :])
    for o in range(plane):
        outs[o][...] = rows[o * depth : (o + 1) * depth].astype(BF16)


def factor_kernel(at_ref, x_ref, gate_own, gate_other, up_own, up_other, *rest):
    out_ref = rest[-1]
    width = gate_own.shape[0]
    core = at_ref[2]
    own = x_ref[:, pl.ds(pl.multiple_of(core * width, 128), width)]
    other = x_ref[:, pl.ds(pl.multiple_of((1 - core) * width, 128), width)]
    gate = dot(own, gate_own[...]) + dot(other, gate_other[...])
    up = dot(own, up_own[...]) + dot(other, up_other[...])
    sig = 1.0 / (1.0 + jnp.exp(-gate))
    silu = gate * sig
    out_ref[0] = (silu * up).astype(BF16)
    out_ref[1] = (up * sig * (1.0 + gate * (1.0 - sig))).astype(BF16)
    out_ref[2] = silu.astype(BF16)


def raw_kernel(plane, count, *refs):
    down_ref = refs[plane * count]
    *rows_refs, full_ref, half_ref = refs[-count - 2 :]
    for i, rows_ref in enumerate(rows_refs):
        rows = stacked([part[...] for part in refs[i * plane : (i + 1) * plane]])
        rows_ref[...] = rows
        raw = dot(rows, down_ref[...])
        size = rows.shape[0]
        full_ref[i * size : (i + 1) * size, :] = raw
        half_ref[i * size : (i + 1) * size, :] = raw.astype(BF16)


def middle_kernel(r, first, plane, depth, at_ref, own_ref, other_ref, mine_ref, theirs_ref, gate_ref, up_ref, *rest):
    *outs, held, sem = rest[-plane - 2 :]
    width = gate_ref.shape[0]
    layer = at_ref[0] ^ r
    half, place = layer // (LAYERS // 2), layer % (LAYERS // 2)

    @pl.when(half == at_ref[2])
    def _():
        pltpu.make_async_copy(mine_ref.at[:, place], held, sem).start()

    @pl.when(half != at_ref[2])
    def _():
        pltpu.make_async_copy(theirs_ref.at[:, place], held, sem).start()

    which = slice(first, first + plane * depth)
    raw = own_ref[which, :] + other_ref[which, :].astype(F32)
    pltpu.make_async_copy(mine_ref.at[:, place], held, sem).wait()
    spots = [at_ref[1] ^ o for o in range(plane)]
    hidden, to_gate, to_up = [
        jnp.concatenate([held[k, spot].astype(F32) for spot in spots], 0) for k in range(3)
    ]
    gate_grad = (raw * to_gate).astype(BF16)
    up_grad = (raw * to_up).astype(BF16)
    for j in range(0, width, TILE):
        cols = slice(j, j + TILE)
        rows = dot(gate_grad, gate_ref[cols, :], COLS_COLS) + dot(up_grad, up_ref[cols, :], COLS_COLS)
        for o in range(plane):
            outs[o][0:depth, cols] = rows[o * depth : (o + 1) * depth].astype(BF16)
    shares = raw * hidden
    lanes = shares[:, 0:128]
    for j in range(128, shares.shape[1], 128):
        lanes = lanes + shares[:, j : j + 128]
    ones = jnp.ones((EXTRA, 128), F32)
    for o in range(plane):
        outs[o][depth : depth + EXTRA, 0:depth] = lax.dot_general(
            ones, lanes[o * depth : (o + 1) * depth], COLS_COLS,
            precision=lax.Precision.HIGHEST, preferred_element_type=F32,
        ).astype(BF16)


def home_sum(plane, depth, at_ref, meta_ref, back, scratch):
    ids, probs = routes_of(meta_ref)
    experts = [at_ref[0] * plane + (at_ref[1] ^ o) for o in range(plane)]
    picks, _ = slot_tables(ids, probs, experts, depth, scratch)
    picks = [pick.astype(BF16) for pick in picks]
    picked = jnp.concatenate([pick.astype(F32) for pick in picks], 0).astype(BF16)
    total = dot(picked, stacked([ref[0:depth, :] for ref in back]), ROWS_ROWS)
    routed = jnp.zeros(ids.shape, F32)
    for ref, expert, pick in zip(back, experts, picks):
        mine = dot(ref[depth : depth + EXTRA, 0:depth], pick)
        routed = routed + jnp.where(ids == expert.astype(F32), mine, 0.0)
    return total, routed, probs


def home_kernel(plane, depth, passed, at_ref, meta_ref, *rest):
    back, out_ref, scratch = rest[:plane], rest[-2 - passed], rest[-1]
    tokens = meta_ref.shape[1]
    total, routed, _ = home_sum(plane, depth, at_ref, meta_ref, back, scratch)
    out_ref[0:tokens, :] = total.astype(BF16)
    out_ref[tokens : tokens + META, 0:tokens] = jnp.concatenate([routed, routed], 0).astype(BF16)


def own_kernel(plane, depth, at_ref, meta_ref, *rest):
    back, (out_ref, routed_ref, scratch) = rest[:plane], rest[-3:]
    out_ref[...], routed_ref[...], _ = home_sum(plane, depth, at_ref, meta_ref, back, scratch)


def final_kernel(meta_ref, own_ref, routed_ref, *rest):
    far, (grad_ref, router_ref) = rest[:3], rest[-2:]
    tokens = meta_ref.shape[1]
    _, probs = routes_of(meta_ref)
    total, routed = own_ref[...], routed_ref[...]
    for ref in far:
        total = total + ref[0:tokens, :].astype(F32)
        routed = routed + ref[tokens : tokens + META, 0:tokens].astype(F32)[0 : routed.shape[0]]
    grad_ref[...] = total.astype(BF16)
    ratio = routed / jnp.where(probs > 0.0, probs, 1.0)
    router_ref[...] = ratio[0 : router_ref.shape[0]].astype(BF16)


def down_kernel(plane, at_ref, *refs):
    rows = refs[:LAYERS]
    mine_ref, theirs_ref = refs[LAYERS : LAYERS + 2]
    out_ref, held, hidden, sem = refs[-4:]
    size = rows[0].shape[0]

    @pl.when(pl.program_id(0) == 0)
    def _():
        half = LAYERS // 2
        copies = [
            pltpu.make_async_copy(mine_ref.at[0], held.at[pl.ds(at_ref[2] * half, half)], sem.at[0]),
            pltpu.make_async_copy(theirs_ref.at[0], held.at[pl.ds((1 - at_ref[2]) * half, half)], sem.at[1]),
        ]
        for copy in copies:
            copy.start()
        for copy in copies:
            copy.wait()
        for r in range(LAYERS):
            hidden[r * size : (r + 1) * size, :] = stacked(
                [held[at_ref[0] ^ r, at_ref[1] ^ o] for o in range(plane)]
            )

    out_ref[...] = dot(jnp.concatenate([ref[...] for ref in rows], 0), hidden[...], ROWS_ROWS)


def body(out_grad, expert_ids, gate_probs, saved_inputs, gate_weight, up_weight, down_weight):
    tokens, width = out_grad.shape
    top = expert_ids.shape[1]
    experts = lax.axis_size("expert")
    plane = experts // LAYERS
    local_rows = saved_inputs.shape[1]
    slots = local_rows * lax.axis_size("fsdp")
    depth = slots // experts
    units = gate_weight.shape[2]
    group = plane * depth
    me = lax.axis_index("expert")
    at = jnp.stack([me // plane, me % plane, lax.axis_index("fsdp")]).astype(jnp.int32)
    gate_own, up_own, down_own = gate_weight[0], up_weight[0], down_weight[0]

    def other_core(array):
        return lax.ppermute(array, "fsdp", [(0, 1), (1, 0)])

    def swapped(array, mask):
        return lax.ppermute(array, "expert", [(e, e ^ mask) for e in range(experts)])

    def other_layer(array, r):
        return swapped(array, r * plane)

    def to_plane(rows):
        return [rows[0]] + [swapped(rows[o], o) for o in range(1, plane)]

    def call(name, kernel, outs, ins, in_specs, out_specs, scratch=(), deps=(), through=(), mib=24, grid=()):
        extra = list(deps) + list(through)
        first = len(ins) + len(deps)
        return pl.pallas_call(
            kernel,
            name=name,
            out_shape=list(outs) + [shape(a.shape, a.dtype) for a in through],
            grid=grid,
            in_specs=list(in_specs) + [ANY] * len(extra),
            out_specs=list(out_specs) + [ANY] * len(through),
            scratch_shapes=list(scratch),
            input_output_aliases={first + i: len(outs) + i for i in range(len(through))},
            compiler_params=params(mib),
            cost_estimate=pl.CostEstimate(flops=COST, bytes_accessed=0, transcendentals=0),
        )(*ins, *extra)

    shape = jax.ShapeDtypeStruct
    table = pltpu.VMEM((max(8, plane), tokens), F32)
    slab = shape((depth, width), BF16)
    longer = shape((depth + EXTRA, width), BF16)
    (pack,) = call(
        "pack",
        pack_kernel,
        [shape((tokens + META, width), BF16)],
        [expert_ids.T, gate_probs.T, out_grad],
        [VMEM] * 3,
        [VMEM],
    )

    def select(block, deps):
        outs = call(
            "select",
            functools.partial(select_kernel, plane, depth),
            [slab] * plane + [shape((META, tokens), BF16)],
            [at, block],
            [SMEM, VMEM],
            [VMEM] * (plane + 1),
            [table],
            deps,
        )
        return outs[:plane], outs[plane]

    def raw_sum(rounds, deps):
        count = len(rounds)
        *rows, full, half = call(
            "raw",
            functools.partial(raw_kernel, plane, count),
            [shape((group, width), BF16)] * count
            + [shape((count * group, units), F32), shape((count * group, units), BF16)],
            [part for r in rounds for part in arrived[r]] + [down_own],
            [VMEM] * (plane * count + 1),
            [VMEM] * (count + 2),
            deps=deps,
        )
        other = other_core(half)
        for i, r in enumerate(rounds):
            raws[r] = rows[i], full, other, i * group
        return full

    def middle(r, raw, deps):
        return call(
            "middle",
            functools.partial(middle_kernel, r, raw[3], plane, depth),
            [longer] * plane,
            [at, raw[1], raw[2], mine, theirs, gate_own, up_own],
            [SMEM, VMEM, VMEM, ANY, ANY, VMEM, VMEM],
            [VMEM] * plane,
            [pltpu.VMEM((3, plane, depth, units), BF16), pltpu.SemaphoreType.DMA],
            deps,
        )

    def home(r, back, deps, through=()):
        out, *passed = call(
            "home",
            functools.partial(home_kernel, plane, depth, len(through)),
            [shape((tokens + META, width), BF16)],
            [at, metas[r], *back],
            [SMEM, VMEM] + [VMEM] * plane,
            [VMEM],
            [table],
            deps,
            through,
        )
        return out, passed

    blocks = [pack, other_layer(pack, 1), other_layer(pack, 2)]
    blocks.append(other_layer(blocks[1], 2))
    gate_other, up_other = other_core(gate_own), other_core(up_own)
    metas = [None] * LAYERS
    rows, metas[0] = select(pack, ())
    arrived = [to_plane(rows), None, None, None]
    factors = []

    def factor(dep):
        j = len(factors)
        whole, part = (lambda i: (0, 0)), (lambda i: (0, j))
        (out,) = pl.pallas_call(
            factor_kernel,
            name="factor",
            out_shape=[shape((3, local_rows, units), BF16)],
            grid=(1,),
            in_specs=[SMEM, pl.BlockSpec((local_rows, 2 * width), whole)]
            + [pl.BlockSpec((width, TILE), part)] * 4
            + [ANY] * (len(dep) + min(j, 1)),
            out_specs=[pl.BlockSpec((3, local_rows, TILE), lambda i: (0, 0, j))],
            input_output_aliases={6 + len(dep): 0} if j else {},
            compiler_params=params(32),
            cost_estimate=pl.CostEstimate(flops=COST, bytes_accessed=0, transcendentals=0),
        )(at, saved_inputs[0], gate_own, gate_other, up_own, up_other, *dep, *factors[-1:])
        factors.append(out)
        return out

    raws, slot_rows = [None] * LAYERS, [None] * LAYERS
    last = rows[0]
    back, far = [None] * LAYERS, [None] * LAYERS
    for kind, r, *awaited in CHAIN:
        seen = [part for w in awaited for part in arrived[w][1:]]
        if kind == "factor":
            last = factor([a for a in [last, *seen] if not any(a is b for b in factors)])
            if len(factors) == units // TILE:
                view = (3, LAYERS // 2, plane, depth, units)
                mine, theirs = last.reshape(view), other_core(last).reshape(view)
        elif kind == "select":
            rows, metas[r] = select(blocks[r], [last, *seen])
            arrived[r] = to_plane(rows)
            last = rows[0]
        elif kind == "raw":
            last = raw_sum(r, [last])
        elif kind == "middle":
            slot_rows[r] = middle(r, raws[r], [last])
            back[r] = to_plane(slot_rows[r])
            last = slot_rows[r][0]
        elif kind == "home":
            last, _ = home(r, back[r], [last])
            far[r] = other_layer(last, r)
        else:
            (down_grad,) = call(
                "down",
                functools.partial(down_kernel, plane),
                [shape((width, units), F32)],
                [at, *[raws[r][0] for r in range(LAYERS)], mine, theirs],
                [SMEM] + [pl.BlockSpec((group, TILE), lambda j: (0, j))] * LAYERS + [ANY, ANY],
                [pl.BlockSpec((TILE, units), lambda j: (j, 0))],
                [
                    pltpu.VMEM((LAYERS, plane, depth, units), BF16),
                    pltpu.VMEM((slots, units), BF16),
                    pltpu.SemaphoreType.DMA((2,)),
                ],
                [last],
                grid=(width // TILE,),
            )
            last = down_grad
    own = call(
        "own",
        functools.partial(own_kernel, plane, depth),
        [shape((tokens, width), F32), shape((8, tokens), F32)],
        [at, metas[0], *back[0]],
        [SMEM] + [VMEM] * (plane + 1),
        [VMEM] * 2,
        [table],
        [last],
    )
    input_grad, router = call(
        "final",
        final_kernel,
        [shape((tokens, width), BF16), shape((top, tokens), BF16)],
        [metas[0], *own, far[1], far[2], far[3]],
        [VMEM] * 6,
        [VMEM] * 2,
    )
    return input_grad, router.T, down_grad[None]


def solution(mesh):
    return jax.shard_map(
        body,
        mesh=mesh,
        in_specs=(
            P("expert", "fsdp"),
            P("expert", None),
            P("expert", None),
            P("expert", "fsdp", None),
            P("expert", "fsdp", None),
            P("expert", "fsdp", None),
            P("expert", "fsdp", None),
        ),
        out_specs=(P("expert", "fsdp"), P("expert", None), P("expert", "fsdp", None)),
        check_vma=False,
    )
```

```python
import functools
import jax
import jax.numpy as jnp
from jax import lax
from jax.experimental import pallas as pl
from jax.experimental.pallas import tpu as pltpu
from jax.sharding import PartitionSpec as P

LAYERS = 4
META = 8
EXTRA = 8
TILE = 256
COSTS = {"pack": 0}
USUAL = 20
CHAIN = (
    ("factor", 0),
    ("factor", 1),
    ("factor", 2),
    ("select", 1, 0),
    ("select", 2),
    ("raw", (2,)),
    ("select", 3, 1),
    ("middle", 2),
    ("raw", (0, 1)),
    ("raw", (3,)),
    ("middle", 3),
    ("home", 2),
    ("middle", 1),
    ("home", 3),
    ("middle", 0),
    ("home", 1),
    ("down", 0),
)
BF16, F32 = jnp.bfloat16, jnp.float32
ROWS_ROWS = (((0,), (0,)), ((), ()))
COLS_COLS = (((1,), (1,)), ((), ()))
VMEM = pl.BlockSpec(memory_space=pltpu.VMEM)
SMEM = pl.BlockSpec(memory_space=pltpu.SMEM)
ANY = pl.BlockSpec(memory_space=pl.ANY)


def dot(a, b, dims=(((1,), (0,)), ((), ()))):
    return lax.dot_general(a, b, dims, preferred_element_type=F32)


def stacked(refs):
    return jnp.concatenate([ref.astype(F32) for ref in refs], 0).astype(BF16)


def cost(name):
    return pl.CostEstimate(flops=COSTS.get(name, USUAL) * 10**9, bytes_accessed=0, transcendentals=0)


def params(mib=24):
    return pltpu.CompilerParams(vmem_limit_bytes=mib * 1024 * 1024)


def pack_kernel(ids_ref, probs_ref, tok_ref, out_ref):
    top, tokens = ids_ref.shape
    width = tok_ref.shape[1]
    none = jnp.full((8 - top, tokens), -1.0, F32)
    ids = jnp.concatenate([ids_ref[...].astype(F32), none], 0)
    probs = jnp.concatenate([probs_ref[...], none], 0)
    meta = jnp.concatenate([ids, probs], 1).astype(BF16)
    out_ref[0:tokens, :] = tok_ref[...]
    out_ref[tokens : tokens + META, :] = jnp.zeros((META, width), BF16)
    out_ref[tokens : tokens + META, 0 : 2 * tokens] = meta


def slot_tables(ids, probs, experts, depth, scratch):
    tokens = ids.shape[1]
    scratch[...] = jnp.zeros_like(scratch)
    weights = []
    for i, expert in enumerate(experts):
        hit = ids == expert.astype(F32)
        scratch[i : i + 1, :] = jnp.max(jnp.where(hit, 1.0, 0.0), axis=0, keepdims=True)
        weights.append(jnp.sum(jnp.where(hit, probs, 0.0), axis=0, keepdims=True))
    before = (
        lax.broadcasted_iota(jnp.int32, (tokens, tokens), 0)
        < lax.broadcasted_iota(jnp.int32, (tokens, tokens), 1)
    ).astype(BF16)
    member = scratch[...]
    rank = jnp.where(member > 0.5, dot(member.astype(BF16), before), -1.0)
    slot = lax.broadcasted_iota(jnp.int32, (depth, tokens), 0).astype(F32)
    picks = [
        jnp.where(jnp.broadcast_to(rank[i : i + 1], slot.shape) == slot, 1.0, 0.0)
        for i in range(len(experts))
    ]
    return picks, weights


def routes_of(meta_ref):
    meta = meta_ref[...].astype(F32)
    tokens = meta_ref.shape[1] // 2
    return meta[:, 0:tokens], meta[:, tokens:]


def select_kernel(plane, depth, at_ref, pack_ref, *rest):
    *outs, meta_ref, scratch = rest[-plane - 2 :]
    tokens = pack_ref.shape[0] - META
    meta_ref[...] = pack_ref[tokens : tokens + META, 0 : 2 * tokens]
    ids, probs = routes_of(meta_ref)
    experts = [at_ref[0] * plane + (at_ref[1] ^ o) for o in range(plane)]
    picks, weights = slot_tables(ids, probs, experts, depth, scratch)
    weighted = jnp.concatenate([p * w for p, w in zip(picks, weights)], 0).astype(BF16)
    rows = dot(weighted, pack_ref[0:tokens, :])
    for o in range(plane):
        outs[o][...] = rows[o * depth : (o + 1) * depth].astype(BF16)


def factor_kernel(at_ref, x_ref, gate_own, gate_other, up_own, up_other, *rest):
    out_ref = rest[-1]
    width = gate_own.shape[0]
    core = at_ref[2]
    own = x_ref[:, pl.ds(pl.multiple_of(core * width, 128), width)]
    other = x_ref[:, pl.ds(pl.multiple_of((1 - core) * width, 128), width)]
    gate = dot(own, gate_own[...]) + dot(other, gate_other[...])
    up = dot(own, up_own[...]) + dot(other, up_other[...])
    sig = 1.0 / (1.0 + jnp.exp(-gate))
    silu = gate * sig
    out_ref[0] = (silu * up).astype(BF16)
    out_ref[1] = (up * sig * (1.0 + gate * (1.0 - sig))).astype(BF16)
    out_ref[2] = silu.astype(BF16)


def raw_kernel(plane, count, *refs):
    down_ref = refs[plane * count]
    *rows_refs, full_ref, half_ref = refs[-count - 2 :]
    for i, rows_ref in enumerate(rows_refs):
        rows = stacked([part[...] for part in refs[i * plane : (i + 1) * plane]])
        rows_ref[...] = rows
        raw = dot(rows, down_ref[...])
        size = rows.shape[0]
        full_ref[i * size : (i + 1) * size, :] = raw
        half_ref[i * size : (i + 1) * size, :] = raw.astype(BF16)


def middle_kernel(r, first, plane, depth, at_ref, own_ref, other_ref, mine_ref, theirs_ref, gate_ref, up_ref, *rest):
    *outs, held, sem = rest[-plane - 2 :]
    width = gate_ref.shape[0]
    layer = at_ref[0] ^ r
    half, place = layer // (LAYERS // 2), layer % (LAYERS // 2)

    @pl.when(half == at_ref[2])
    def _():
        pltpu.make_async_copy(mine_ref.at[:, place], held, sem).start()

    @pl.when(half != at_ref[2])
    def _():
        pltpu.make_async_copy(theirs_ref.at[:, place], held, sem).start()

    which = slice(first, first + plane * depth)
    raw = own_ref[which, :] + other_ref[which, :].astype(F32)
    pltpu.make_async_copy(mine_ref.at[:, place], held, sem).wait()
    spots = [at_ref[1] ^ o for o in range(plane)]
    hidden, to_gate, to_up = [
        jnp.concatenate([held[k, spot].astype(F32) for spot in spots], 0) for k in range(3)
    ]
    gate_grad = (raw * to_gate).astype(BF16)
    up_grad = (raw * to_up).astype(BF16)
    for j in range(0, width, TILE):
        cols = slice(j, j + TILE)
        rows = dot(gate_grad, gate_ref[cols, :], COLS_COLS) + dot(up_grad, up_ref[cols, :], COLS_COLS)
        for o in range(plane):
            outs[o][0:depth, cols] = rows[o * depth : (o + 1) * depth].astype(BF16)
    shares = raw * hidden
    lanes = shares[:, 0:128]
    for j in range(128, shares.shape[1], 128):
        lanes = lanes + shares[:, j : j + 128]
    ones = jnp.ones((EXTRA, 128), F32)
    for o in range(plane):
        outs[o][depth : depth + EXTRA, 0:depth] = lax.dot_general(
            ones, lanes[o * depth : (o + 1) * depth], COLS_COLS,
            precision=lax.Precision.HIGHEST, preferred_element_type=F32,
        ).astype(BF16)


def home_sum(plane, depth, at_ref, meta_ref, back, scratch):
    ids, probs = routes_of(meta_ref)
    experts = [at_ref[0] * plane + (at_ref[1] ^ o) for o in range(plane)]
    picks, _ = slot_tables(ids, probs, experts, depth, scratch)
    picks = [pick.astype(BF16) for pick in picks]
    picked = jnp.concatenate([pick.astype(F32) for pick in picks], 0).astype(BF16)
    total = dot(picked, stacked([ref[0:depth, :] for ref in back]), ROWS_ROWS)
    routed = jnp.zeros(ids.shape, F32)
    for ref, expert, pick in zip(back, experts, picks):
        mine = dot(ref[depth : depth + EXTRA, 0:depth], pick)
        routed = routed + jnp.where(ids == expert.astype(F32), mine, 0.0)
    return total, routed, probs


def home_kernel(plane, depth, passed, at_ref, meta_ref, *rest):
    back, out_ref, scratch = rest[:plane], rest[-2 - passed], rest[-1]
    tokens = meta_ref.shape[1] // 2
    total, routed, _ = home_sum(plane, depth, at_ref, meta_ref, back, scratch)
    out_ref[0:tokens, :] = total.astype(BF16)
    out_ref[tokens : tokens + META, 0:tokens] = routed.astype(BF16)


def own_kernel(plane, depth, at_ref, meta_ref, *rest):
    back, (out_ref, routed_ref, scratch) = rest[:plane], rest[-3:]
    out_ref[...], routed_ref[...], _ = home_sum(plane, depth, at_ref, meta_ref, back, scratch)


def final_kernel(meta_ref, own_ref, routed_ref, *rest):
    far, (grad_ref, router_ref) = rest[:3], rest[-2:]
    tokens = meta_ref.shape[1] // 2
    _, probs = routes_of(meta_ref)
    total, routed = own_ref[...], routed_ref[...]
    for ref in far:
        total = total + ref[0:tokens, :].astype(F32)
        routed = routed + ref[tokens : tokens + META, 0:tokens].astype(F32)
    grad_ref[...] = total.astype(BF16)
    ratio = routed / jnp.where(probs > 0.0, probs, 1.0)
    router_ref[...] = ratio[0 : router_ref.shape[0]].astype(BF16)


def down_kernel(plane, at_ref, *refs):
    rows = refs[:LAYERS]
    mine_ref, theirs_ref = refs[LAYERS : LAYERS + 2]
    out_ref, held, hidden, sem = refs[-4:]
    size = rows[0].shape[0]

    @pl.when(pl.program_id(0) == 0)
    def _():
        half = LAYERS // 2
        copies = [
            pltpu.make_async_copy(mine_ref.at[0], held.at[pl.ds(at_ref[2] * half, half)], sem.at[0]),
            pltpu.make_async_copy(theirs_ref.at[0], held.at[pl.ds((1 - at_ref[2]) * half, half)], sem.at[1]),
        ]
        for copy in copies:
            copy.start()
        for copy in copies:
            copy.wait()
        for r in range(LAYERS):
            hidden[r * size : (r + 1) * size, :] = stacked(
                [held[at_ref[0] ^ r, at_ref[1] ^ o] for o in range(plane)]
            )

    out_ref[...] = dot(jnp.concatenate([ref[...] for ref in rows], 0), hidden[...], ROWS_ROWS)


def body(out_grad, expert_ids, gate_probs, saved_inputs, gate_weight, up_weight, down_weight):
    tokens, width = out_grad.shape
    top = expert_ids.shape[1]
    experts = lax.axis_size("expert")
    plane = experts // LAYERS
    local_rows = saved_inputs.shape[1]
    slots = local_rows * lax.axis_size("fsdp")
    depth = slots // experts
    units = gate_weight.shape[2]
    group = plane * depth
    me = lax.axis_index("expert")
    at = jnp.stack([me // plane, me % plane, lax.axis_index("fsdp")]).astype(jnp.int32)
    gate_own, up_own, down_own = gate_weight[0], up_weight[0], down_weight[0]

    def other_core(array):
        return lax.ppermute(array, "fsdp", [(0, 1), (1, 0)])

    def swapped(array, mask):
        return lax.ppermute(array, "expert", [(e, e ^ mask) for e in range(experts)])

    def other_layer(array, r):
        return swapped(array, r * plane)

    def to_plane(rows):
        return [rows[0]] + [swapped(rows[o], o) for o in range(1, plane)]

    def call(name, kernel, outs, ins, in_specs, out_specs, scratch=(), deps=(), through=(), mib=24, grid=()):
        extra = list(deps) + list(through)
        first = len(ins) + len(deps)
        return pl.pallas_call(
            kernel,
            name=name,
            out_shape=list(outs) + [shape(a.shape, a.dtype) for a in through],
            grid=grid,
            in_specs=list(in_specs) + [ANY] * len(extra),
            out_specs=list(out_specs) + [ANY] * len(through),
            scratch_shapes=list(scratch),
            input_output_aliases={first + i: len(outs) + i for i in range(len(through))},
            compiler_params=params(mib),
            cost_estimate=cost(name),
        )(*ins, *extra)

    shape = jax.ShapeDtypeStruct
    table = pltpu.VMEM((max(8, plane), tokens), F32)
    slab = shape((depth, width), BF16)
    longer = shape((depth + EXTRA, width), BF16)
    (pack,) = call(
        "pack",
        pack_kernel,
        [shape((tokens + META, width), BF16)],
        [expert_ids.T, gate_probs.T, out_grad],
        [VMEM] * 3,
        [VMEM],
    )

    def select(r, deps):
        outs = call(
            "select%d" % r,
            functools.partial(select_kernel, plane, depth),
            [slab] * plane + [shape((META, 2 * tokens), BF16)],
            [at, blocks[r]],
            [SMEM, VMEM],
            [VMEM] * (plane + 1),
            [table],
            deps,
        )
        return outs[:plane], outs[plane]

    def raw_sum(rounds, deps):
        count = len(rounds)
        *rows, full, half = call(
            "raw%d" % rounds[0],
            functools.partial(raw_kernel, plane, count),
            [shape((group, width), BF16)] * count
            + [shape((count * group, units), F32), shape((count * group, units), BF16)],
            [part for r in rounds for part in arrived[r]] + [down_own],
            [VMEM] * (plane * count + 1),
            [VMEM] * (count + 2),
            deps=deps,
        )
        other = other_core(half)
        for i, r in enumerate(rounds):
            raws[r] = rows[i], full, other, i * group
        return full

    def middle(r, raw, deps):
        return call(
            "middle%d" % r,
            functools.partial(middle_kernel, r, raw[3], plane, depth),
            [longer] * plane,
            [at, raw[1], raw[2], mine, theirs, gate_own, up_own],
            [SMEM, VMEM, VMEM, ANY, ANY, VMEM, VMEM],
            [VMEM] * plane,
            [pltpu.VMEM((3, plane, depth, units), BF16), pltpu.SemaphoreType.DMA],
            deps,
        )

    def home(r, back, deps, through=()):
        out, *passed = call(
            "home%d" % r,
            functools.partial(home_kernel, plane, depth, len(through)),
            [shape((tokens + META, width), BF16)],
            [at, metas[r], *back],
            [SMEM, VMEM] + [VMEM] * plane,
            [VMEM],
            [table],
            deps,
            through,
        )
        return out, passed

    blocks = [pack, other_layer(pack, 1), other_layer(pack, 2)]
    blocks.append(other_layer(pack, 3))
    gate_other, up_other = other_core(gate_own), other_core(up_own)
    metas = [None] * LAYERS
    rows, metas[0] = select(0, ())
    arrived = [to_plane(rows), None, None, None]
    factors = []

    def factor(dep):
        j = len(factors)
        name = "factor%d" % j
        whole, part = (lambda i: (0, 0)), (lambda i: (0, j))
        (out,) = pl.pallas_call(
            factor_kernel,
            name=name,
            out_shape=[shape((3, local_rows, units), BF16)],
            grid=(1,),
            in_specs=[SMEM, pl.BlockSpec((local_rows, 2 * width), whole)]
            + [pl.BlockSpec((width, TILE), part)] * 4
            + [ANY] * (len(dep) + min(j, 1)),
            out_specs=[pl.BlockSpec((3, local_rows, TILE), lambda i: (0, 0, j))],
            input_output_aliases={6 + len(dep): 0} if j else {},
            compiler_params=params(32),
            cost_estimate=cost(name),
        )(at, saved_inputs[0], gate_own, gate_other, up_own, up_other, *dep, *factors[-1:])
        factors.append(out)
        return out

    raws, slot_rows = [None] * LAYERS, [None] * LAYERS
    last = rows[0]
    back, far = [None] * LAYERS, [None] * LAYERS
    for kind, r, *awaited in CHAIN:
        seen = [part for w in awaited for part in (arrived[w][1:] if w < LAYERS else [far[w - LAYERS]])]
        if kind == "factor":
            last = factor([a for a in [last, *seen] if not any(a is b for b in factors)])
            if len(factors) == units // TILE:
                view = (3, LAYERS // 2, plane, depth, units)
                mine, theirs = last.reshape(view), other_core(last).reshape(view)
        elif kind == "select":
            rows, metas[r] = select(r, [last, *seen])
            arrived[r] = to_plane(rows)
            last = rows[0]
        elif kind == "raw":
            last = raw_sum(r, [last])
        elif kind == "middle":
            slot_rows[r] = middle(r, raws[r], [last])
            back[r] = to_plane(slot_rows[r])
            last = slot_rows[r][0]
        elif kind == "home":
            last, _ = home(r, back[r], [last, *seen])
            far[r] = other_layer(last, r)
        else:
            (down_grad,) = call(
                "down",
                functools.partial(down_kernel, plane),
                [shape((width, units), F32)],
                [at, *[raws[r][0] for r in range(LAYERS)], mine, theirs],
                [SMEM] + [pl.BlockSpec((group, TILE), lambda j: (0, j))] * LAYERS + [ANY, ANY],
                [pl.BlockSpec((TILE, units), lambda j: (j, 0))],
                [
                    pltpu.VMEM((LAYERS, plane, depth, units), BF16),
                    pltpu.VMEM((slots, units), BF16),
                    pltpu.SemaphoreType.DMA((2,)),
                ],
                [last, *seen],
                grid=(width // TILE,),
            )
            last = down_grad
    own = call(
        "own",
        functools.partial(own_kernel, plane, depth),
        [shape((tokens, width), F32), shape((8, tokens), F32)],
        [at, metas[0], *back[0]],
        [SMEM] + [VMEM] * (plane + 1),
        [VMEM] * 2,
        [table],
        [last],
    )
    input_grad, router = call(
        "final",
        final_kernel,
        [shape((tokens, width), BF16), shape((top, tokens), BF16)],
        [metas[0], *own, far[1], far[2], far[3]],
        [VMEM] * 6,
        [VMEM] * 2,
    )
    return input_grad, router.T, down_grad[None]


def solution(mesh):
    return jax.shard_map(
        body,
        mesh=mesh,
        in_specs=(
            P("expert", "fsdp"),
            P("expert", None),
            P("expert", None),
            P("expert", "fsdp", None),
            P("expert", "fsdp", None),
            P("expert", "fsdp", None),
            P("expert", "fsdp", None),
        ),
        out_specs=(P("expert", "fsdp"), P("expert", None), P("expert", "fsdp", None)),
        check_vma=False,
    )
```
